256 devices in a mesh: unit: 16 (over x_lo, y, core), feat: 8 (over z), tm: 2 (over x_hi).
Axes of the slice: x: 4 (x_hi: 2, x_lo: 2; x = x_hi * 2 + x_lo), y: 4, z: 8, core: 2. Of those that a mesh axis runs over, the one named last changes fastest.
Arguments:
- tensor: bfloat16 [32, 16384, 2048], P('tm', 'unit', 'feat'), may hold values from -6 to 6
- unit_factor: float32 [16384, 64], P(('unit', 'feat', 'tm')), may hold values from -0.32 to 0.32
- window_factor: float32 [32, 64], P('tm'), may hold values from -1.5 to 1.5
- feat_factor: float32 [2048, 64], P(('feat', 'tm')), may hold values from -0.32 to 0.32
Outputs:
- grad_unit: float32 [16384, 64], P(('unit', 'feat', 'tm'))
- grad_window: float32 [32, 64], P('tm')
- grad_feat: float32 [2048, 64], P(('feat', 'tm'))
The draws below stay inside these ranges and needn't reach their ends.
All inputs are finite; a program needn't handle non-finite values.
Results may differ from the reference program's by a relative error of at most 0.0065.
Values may be sent and summed in bfloat16 or wider, within the bound.
No kernel may reach another device: no remote copies, remote signals or barrier semaphores. Data moves between devices by JAX's collectives and lax.ppermute only.
A program may use at most 64 MiB of HBM per device.

```python
import math
import jax
import jax.numpy as jnp
from jax import lax

RANK = 64
FEATS = 2048
UNIT_DEV = 1024
UNITS = 16384
WINDOWS = 32


def rising_rows(key, count, width):
    position = jnp.arange(count, dtype=jnp.float32) / count
    scale = 0.06 * 3.0 ** (position - 0.5)
    base = jax.random.truncated_normal(key, -3.0, 3.0, (count, width), jnp.float32)
    return base * scale[:, None]


def draw_unit_factor(key, part):
    key = jax.random.fold_in(key, 11)
    return rising_rows(key, UNITS, RANK)


def draw_feat_factor(key, part):
    key = jax.random.fold_in(key, 12)
    return rising_rows(key, FEATS, RANK)


def shard_levels(key, dims, split, smallest, top_value):
    factor_of = 1.0
    for axis_at, shards_of in split:
        heights = jax.random.uniform(jax.random.fold_in(jax.random.fold_in(key, 6), axis_at), (shards_of,), jnp.float32, smallest / len(split), top_value / len(split))
        factor_of = factor_of * jnp.repeat(jnp.exp(heights), dims[axis_at] // shards_of).reshape((-1,) + (1,) * (len(dims) - 1 - axis_at))
    return factor_of


def normal_values(key, shape, scale, most, cuts=(), held_as=jnp.bfloat16):
    loudness = shard_levels(key, shape, cuts, -0.22, 0.18) if cuts else 1.0
    array = jax.random.normal(key, shape, jnp.float32) * scale * loudness
    return jnp.minimum(jnp.maximum(array, -most), most).astype(held_as)


def setup_inputs(seed: int = 0) -> dict:
    keys = jax.random.split(jax.random.key(seed), 5)
    tensor = normal_values(keys[0], (WINDOWS, UNITS, FEATS), 1.0, 6.0, ((0, 2), (1, 16), (2, 8)))
    unit_factor = draw_unit_factor(jax.random.fold_in(keys[4], 71), 0)
    window_factor = normal_values(keys[2], (WINDOWS, RANK), 0.3, 1.5, ((0, 2),), jnp.float32)
    feat_factor = draw_feat_factor(jax.random.fold_in(keys[4], 71), 0)
    return dict(tensor=tensor, unit_factor=unit_factor, window_factor=window_factor, feat_factor=feat_factor)


def reference(tensor, unit_factor, window_factor, feat_factor):
    high = lax.Precision.HIGHEST
    unit_wide = unit_factor.astype(jnp.bfloat16).astype(jnp.float32)
    window_wide = window_factor.astype(jnp.bfloat16).astype(jnp.float32)
    feat_wide = feat_factor.astype(jnp.bfloat16).astype(jnp.float32)
    block = UNIT_DEV
    steps_count = UNITS // block

    def step(carry, index):
        by_window, by_feat = carry
        start = (index * block).astype(jnp.int32)
        slab = lax.dynamic_slice_in_dim(tensor, start, block, 1).astype(jnp.float32)
        unit_rows = lax.dynamic_slice_in_dim(unit_wide, start, block, 0)
        first = jnp.einsum('jik,kr->jir', slab, feat_wide)
        along = jnp.einsum('jir,jr->ir', first, window_wide)
        by_window = by_window + jnp.einsum('jir,ir->jr', first, unit_rows)
        second = jnp.einsum('jik,ir->jkr', slab, unit_rows)
        by_feat = by_feat + jnp.einsum('jkr,jr->kr', second, window_wide)
        return ((by_window, by_feat), along)
    init = (jnp.zeros((WINDOWS, RANK), jnp.float32), jnp.zeros((FEATS, RANK), jnp.float32))
    (by_window, by_feat), pieces = lax.scan(step, init, jnp.arange(steps_count, dtype=jnp.int32))
    by_unit = pieces.reshape(UNITS, RANK)
    gram_unit = jnp.dot(unit_factor.T, unit_factor, precision=high, preferred_element_type=jnp.float32)
    gram_window = jnp.dot(window_factor.T, window_factor, precision=high, preferred_element_type=jnp.float32)
    gram_feat = jnp.dot(feat_factor.T, feat_factor, precision=high, preferred_element_type=jnp.float32)
    grad_unit = (jnp.dot(unit_factor, gram_window * gram_feat, precision=high, preferred_element_type=jnp.float32) - by_unit) / math.sqrt(WINDOWS * FEATS)
    grad_window = (jnp.dot(window_factor, gram_unit * gram_feat, precision=high, preferred_element_type=jnp.float32) - by_window) / math.sqrt(UNITS * FEATS)
    grad_feat = (jnp.dot(feat_factor, gram_unit * gram_window, precision=high, preferred_element_type=jnp.float32) - by_feat) / math.sqrt(UNITS * WINDOWS)
    return (grad_unit, grad_window, grad_feat)
```

```python
import functools
import math

import jax
import jax.numpy as jnp
from jax import lax
from jax.experimental import pallas as pl
from jax.experimental.pallas import tpu as pltpu
from jax.sharding import PartitionSpec as P

F32 = jnp.float32
BF16 = jnp.bfloat16
HIGH = lax.Precision.HIGHEST
NT = (((1,), (1,)), ((), ()))
TN = (((0,), (0,)), ((), ()))
GROUP = ("feat", "tm")
VMEM = pl.BlockSpec(memory_space=pltpu.VMEM)
HBM = pl.BlockSpec(memory_space=pltpu.HBM)


def call(kernel, out_shape, *args, name, far=(), **more):
    args = [
        pltpu.with_memory_space_constraint(arg, pltpu.HBM) if at in far else arg
        for at, arg in enumerate(args)
    ]
    return pl.pallas_call(
        kernel,
        out_shape=out_shape,
        in_specs=[HBM if at in far else VMEM for at in range(len(args))],
        out_specs=jax.tree.map(lambda _: VMEM, out_shape),
        compiler_params=pltpu.CompilerParams(vmem_limit_bytes=16 * 2**20),
        name=name,
        **more,
    )(*args)


def spread(rows):
    half = rows.shape[0] // 2
    return jnp.concatenate([rows[:half], rows[half:]], axis=-1)


def stack(rows):
    return jnp.concatenate([rows[:, :64], rows[:, 64:]], axis=0)


def low(value):
    return value.astype(BF16).astype(F32)


def split(value, axis):
    high_part = low(value)
    return jnp.concatenate([high_part, low(value - high_part)], axis=axis)


def dot(one, two):
    return jnp.dot(one, two, precision=HIGH, preferred_element_type=F32)


def prepare_kernel(
    unit_far, feat_far, window_far, gather_ref, pair_ref, feat_ref, window_ref, unit_ref, sems
):
    copies = [
        pltpu.make_async_copy(unit_far, unit_ref, sems.at[0]),
        pltpu.make_async_copy(feat_far, feat_ref, sems.at[1]),
        pltpu.make_async_copy(window_far, window_ref, sems.at[2]),
    ]
    for copy in copies:
        copy.start()
    copies[1].wait()
    copies[2].wait()
    parts = [split(feat_ref[...], 0), split(window_ref[...], -1)]
    pair_ref[...] = jnp.concatenate(parts, axis=0).astype(BF16)
    copies[0].wait()
    chunk = spread(unit_ref[...].T).astype(BF16)
    for at in range(16):
        gather_ref[at] = chunk


def fetches(tensor_far, places, sems, halved):
    rows = tensor_far.shape[1] // 2
    result, at = [], 0
    for window, place in places:
        parts = 2 if len(result) < halved else 1
        copies = []
        for part in range(parts):
            span = pl.ds(part * rows, rows * 2 // parts)
            source, target = tensor_far.at[window, span], place.at[span]
            copies.append(pltpu.make_async_copy(source, target, sems.at[at]))
            at += 1
        result.append(copies)
    for copies in result:
        for copy in copies:
            copy.start()
    return result


def unit_kernel(
    tensor_far, pair_ref, feat_ref, window_ref,
    kept_ref, out_ref, both_ref, gram_ref, tensor_ref, total, sems,
):
    windows, kept = tensor_far.shape[0], kept_ref.shape[0]
    places = [
        (j, kept_ref.at[j] if j < kept else tensor_ref.at[j - kept]) for j in range(windows)
    ]
    copies = fetches(tensor_far, places, sems, windows // 2)
    pair = pair_ref[0:128].astype(F32)
    mine, other = feat_ref[...], pair[0:64] + pair[64:128]
    first = lax.axis_index("tm") == 0
    feat = jnp.concatenate(
        [jnp.where(first, mine, other), jnp.where(first, other, mine)], axis=-1
    )
    gram = lax.dot_general(feat, feat, NT, precision=HIGH, preferred_element_type=F32)
    place = lax.broadcasted_iota(jnp.int32, (64, 64), 0) // 16 == lax.axis_index("unit") // 4
    gram = jnp.sum(jnp.where(place, gram, 0.0).reshape(4, 16, 64), axis=0)
    gram_ref[...] = split(gram, -1).astype(BF16)
    both_ref[...] = low(feat)
    feat = feat.astype(BF16)
    window = low(window_ref[...]).T
    for j in range(windows):
        for copy in copies[j]:
            copy.wait()
        part = lax.dot_general(feat, places[j][1][...], NT, preferred_element_type=F32)
        part = part * window[:, j : j + 1]
        if j == 0:
            total[...] = part
        else:
            total[...] += part
    left = lax.broadcasted_iota(jnp.int32, (32, 128), 1) < 64
    for at in range(0, 16, 2):
        top = total[0:32, at * 64 : at * 64 + 128]
        bottom = total[32:64, at * 64 : at * 64 + 128]
        out_ref[at] = jnp.where(left, top, pltpu.roll(bottom, 64, 1)).astype(BF16)
        out_ref[at + 1] = jnp.where(left, pltpu.roll(top, 64, 1), bottom).astype(BF16)


def feature_kernel(
    tensor_far, kept_ref, gather_ref, both_ref, window_ref,
    sums_ref, tensor_ref, unit_ref, total, products, sems,
):
    windows, kept = tensor_far.shape[0], kept_ref.shape[0]
    places = [(j, tensor_ref.at[j - kept]) for j in range(kept, windows)]
    copies = fetches(tensor_far, places, sems, (windows - kept) // 2)
    left = lax.broadcasted_iota(jnp.int32, (32, 128), 1) < 64
    for at in range(0, 16, 2):
        one = gather_ref[at].astype(F32)
        two = gather_ref[at + 1].astype(F32)
        columns = pl.ds(at * 64, 128)
        unit_ref[0:32, columns] = jnp.where(left, one, pltpu.roll(two, 64, 1)).astype(BF16)
        unit_ref[32:64, columns] = jnp.where(left, pltpu.roll(one, 64, 1), two).astype(BF16)
    unit = unit_ref[...]
    feat = both_ref[...]
    window = low(window_ref[...]).T
    for j in range(windows):
        if j < kept:
            slab = kept_ref[j]
        else:
            for copy in copies[j - kept]:
                copy.wait()
            slab = tensor_ref[j - kept]
        second = jnp.dot(unit, slab, preferred_element_type=F32)
        product = second * feat
        products[j] = product[:, :128] + product[:, 128:]
        second = second * window[:, j : j + 1]
        if j == 0:
            total[...] = second
        else:
            total[...] += second
    gram = lax.dot_general(unit, unit, NT, preferred_element_type=F32)
    rest = jnp.concatenate([spread(gram), spread(jnp.sum(products[...], axis=-1))], axis=0)
    parts = [total[:, :128], total[:, 128:], split(rest, 0)]
    sums_ref[...] = jnp.concatenate(parts, axis=0).astype(BF16)


def add_four(refs):
    one, two, three, four = [ref[...].astype(F32) for ref in refs]
    return (one + two) + (three + four)


def near_kernel(s0, s1, s2, s3, by_unit_ref, gram_ref, scatter_ref, send_ref, keep_ref):
    total = add_four((s0, s1, s2, s3))
    rest = total[128:168] + total[168:208]
    tm = lax.axis_index("tm")
    first = tm == 0
    send_ref[...] = jnp.where(first, total[64:128], total[0:64])
    keep_ref[0:64] = jnp.where(first, total[0:64], total[64:128])
    keep_ref[64:96] = rest[0:32]
    by_window = split(rest[32:40], 0)
    gram = gram_ref[...].astype(F32)
    for at in range(16):
        scatter_ref[at, 0:32] = by_unit_ref[at]
        scatter_ref[at, 32:48] = jnp.where(tm == at % 2, by_window, gram).astype(BF16)


def group_kernel(scatter_ref, keep_ref, other_ref, unit_ref, sums_ref):
    even = scatter_ref[0].astype(F32)
    odd = scatter_ref[1].astype(F32)
    for at in range(2, 16, 2):
        even += scatter_ref[at].astype(F32)
        odd += scatter_ref[at + 1].astype(F32)
    unit_ref[...] = even[0:32] + odd[0:32]
    first = lax.axis_index("tm") == 0
    by_window = jnp.where(first, even[32:48], odd[32:48])
    gram = jnp.where(first, odd[32:48], even[32:48])
    gram = jnp.concatenate([gram[:, :64] + gram[:, 64:]] * 4, axis=0)
    place = lax.broadcasted_iota(jnp.int32, (64, 64), 0) // 16 == lax.axis_index("unit") // 4
    sums_ref[0:64] = keep_ref[0:64] + other_ref[...]
    sums_ref[64:96] = keep_ref[64:96]
    sums_ref[96:128] = spread(jnp.where(place, gram, 0.0))
    sums_ref[128:136] = by_window[0:8] + by_window[8:16]


def gradient_kernel(
    scales, s0, s1, s2, s3, by_unit_ref, unit_ref, window_ref, feat_ref, pair_ref,
    grad_unit_ref, grad_window_ref, grad_feat_ref,
):
    total = add_four((s0, s1, s2, s3))
    gram_unit, gram_feat = stack(total[64:96]), stack(total[96:128])
    window = window_ref[...]
    other = pair_ref[128:144, :].astype(F32)
    other = other[:, :64] + other[:, 64:]
    windows = jnp.concatenate([window, other], axis=0)
    gram_window = lax.dot_general(
        windows, windows, TN, precision=HIGH, preferred_element_type=F32
    )
    grad_unit_ref[...] = (
        dot(unit_ref[...], gram_window * gram_feat) - stack(by_unit_ref[...]).T
    ) * scales[0]
    grad_window_ref[...] = (
        dot(window, gram_unit * gram_feat) - stack(total[128:136])
    ) * scales[1]
    grad_feat_ref[...] = (dot(gram_unit * gram_window, feat_ref[...]) - total[0:64]) * scales[2]


def by_xor(value, mask):
    count = lax.axis_size("unit")
    return lax.ppermute(value, "unit", [(i, i ^ mask) for i in range(count)])


def body(tensor, unit_factor, window_factor, feat_factor):
    win_rows, unit_count, feat_count = tensor.shape
    units_all = unit_count * lax.axis_size("unit")
    windows_all = win_rows * lax.axis_size("tm")
    feats_all = feat_count * lax.axis_size("feat")
    shape = jax.ShapeDtypeStruct
    feat = feat_factor.T
    gather, pair, feat_near, window_near = call(
        prepare_kernel,
        [
            shape((16, 32, 128), BF16),
            shape((144, 128), BF16),
            shape((64, 128), F32),
            shape((win_rows, 64), F32),
        ],
        unit_factor, feat, window_factor,
        far=(0, 1, 2),
        scratch_shapes=[pltpu.VMEM((64, 64), F32), pltpu.SemaphoreType.DMA((3,))],
        name="prepare",
    )
    pair = lax.ppermute(pair, "tm", [(0, 1), (1, 0)])
    gather = lax.all_to_all(gather.reshape(512, 128), GROUP, 0, 0, tiled=True).reshape(16, 32, 128)
    cost = pl.CostEstimate(flops=2**33, bytes_accessed=2**23, transcendentals=0)
    kept = 6
    kept_windows, by_unit, both, gram = call(
        unit_kernel,
        [
            pltpu.VMEM((kept, unit_count, feat_count), BF16),
            shape((16, 32, 128), BF16),
            shape((64, feat_count), F32),
            shape((16, 128), BF16),
        ],
        tensor, pair, feat_near, window_near,
        far=(0,),
        scratch_shapes=[
            pltpu.VMEM((win_rows - kept, unit_count, feat_count), BF16),
            pltpu.VMEM((64, unit_count), F32),
            pltpu.SemaphoreType.DMA((2 * win_rows,)),
        ],
        cost_estimate=cost,
        name="by_unit",
    )
    sums = call(
        feature_kernel,
        shape((208, 128), BF16),
        tensor, pltpu.with_memory_space_constraint(kept_windows, pltpu.VMEM), gather, both, window_near,
        far=(0,),
        scratch_shapes=[
            pltpu.VMEM((win_rows - kept, unit_count, feat_count), BF16),
            pltpu.VMEM((64, unit_count), BF16),
            pltpu.VMEM((64, feat_count), F32),
            pltpu.VMEM((win_rows, 64, 128), F32),
            pltpu.SemaphoreType.DMA((2 * win_rows,)),
        ],
        cost_estimate=cost,
        name="by_feature",
    )
    near = [by_xor(sums, mask) for mask in (1, 2, 3)]
    scatter, send, keep = call(
        near_kernel,
        [shape((16, 48, 128), BF16), shape((64, 128), F32), shape((96, 128), F32)],
        sums, *near, by_unit, gram,
        name="near_sums",
    )
    other = lax.ppermute(send, "tm", [(0, 1), (1, 0)])
    scatter = lax.all_to_all(scatter.reshape(768, 128), GROUP, 0, 0, tiled=True).reshape(16, 48, 128)
    by_unit, sums = call(
        group_kernel,
        [shape((32, 128), F32), shape((136, 128), F32)],
        scatter, keep, other,
        name="group_sums",
    )
    far = [by_xor(sums, mask) for mask in (8, 4, 12)]
    scales = (
        1 / math.sqrt(windows_all * feats_all),
        1 / math.sqrt(units_all * feats_all),
        1 / math.sqrt(units_all * windows_all),
    )
    grad_unit, grad_window, grad_feat = call(
        functools.partial(gradient_kernel, scales),
        [shape((64, 64), F32), shape((win_rows, 64), F32), shape((64, 128), F32)],
        sums, *far, by_unit, unit_factor, window_factor, feat, pair,
        name="gradients",
    )
    return grad_unit, grad_window, grad_feat.T


def solution(mesh):
    in_specs = (
        P("tm", "unit", "feat"),
        P(("unit", "feat", "tm"), None),
        P("tm", None),
        P(("feat", "tm"), None),
    )
    out_specs = (P(("unit", "feat", "tm"), None), P("tm", None), P(("feat", "tm"), None))
    return jax.shard_map(body, mesh=mesh, in_specs=in_specs, out_specs=out_specs, check_vma=False)
```

```python
import functools
import math

import jax
import jax.numpy as jnp
from jax import lax
from jax.experimental import pallas as pl
from jax.experimental.pallas import tpu as pltpu
from jax.sharding import PartitionSpec as P

F32 = jnp.float32
BF16 = jnp.bfloat16
HIGH = lax.Precision.HIGHEST
NT = (((1,), (1,)), ((), ()))
TN = (((0,), (0,)), ((), ()))
GROUP = ("feat", "tm")
VMEM = pl.BlockSpec(memory_space=pltpu.VMEM)
HBM = pl.BlockSpec(memory_space=pltpu.HBM)


def call(kernel, out_shape, *args, name, far=(), **more):
    args = [
        pltpu.with_memory_space_constraint(arg, pltpu.HBM) if at in far else arg
        for at, arg in enumerate(args)
    ]
    return pl.pallas_call(
        kernel,
        out_shape=out_shape,
        in_specs=[HBM if at in far else VMEM for at in range(len(args))],
        out_specs=jax.tree.map(lambda _: VMEM, out_shape),
        compiler_params=pltpu.CompilerParams(vmem_limit_bytes=16 * 2**20),
        name=name,
        **more,
    )(*args)


def spread(rows):
    half = rows.shape[0] // 2
    return jnp.concatenate([rows[:half], rows[half:]], axis=-1)


def stack(rows):
    return jnp.concatenate([rows[:, :64], rows[:, 64:]], axis=0)


def low(value):
    return value.astype(BF16).astype(F32)


def split(value, axis):
    high_part = low(value)
    return jnp.concatenate([high_part, low(value - high_part)], axis=axis)


def dot(one, two):
    return jnp.dot(one, two, precision=HIGH, preferred_element_type=F32)


def prepare_kernel(
    unit_far, feat_far, window_far, gather_ref, pair_ref, feat_ref, window_ref, unit_ref, sems
):
    copies = [
        pltpu.make_async_copy(unit_far, unit_ref, sems.at[0]),
        pltpu.make_async_copy(feat_far, feat_ref, sems.at[1]),
        pltpu.make_async_copy(window_far, window_ref, sems.at[2]),
    ]
    for copy in copies:
        copy.start()
    copies[1].wait()
    copies[2].wait()
    parts = [split(feat_ref[...], 0), split(window_ref[...], -1)]
    pair_ref[...] = jnp.concatenate(parts, axis=0).astype(BF16)
    copies[0].wait()
    chunk = spread(unit_ref[...].T).astype(BF16)
    for at in range(16):
        gather_ref[at] = chunk


def fetches(tensor_far, places, sems):
    rows = tensor_far.shape[1] // 2
    result = []
    for at, (window, place) in enumerate(places):
        copies = []
        for part in range(2):
            span = pl.ds(part * rows, rows)
            source, target = tensor_far.at[window, span], place.at[span]
            copies.append(pltpu.make_async_copy(source, target, sems.at[2 * at + part]))
        result.append(copies)
    return result


def start(batch):
    for copies in batch:
        for copy in copies:
            copy.start()


def add_to(total, part, fresh):
    if fresh:
        total[...] = part
    else:
        total[...] += part


def by_unit_part(feat, slab, window, j):
    part = lax.dot_general(feat, slab, NT, preferred_element_type=F32)
    return part * window[:, j : j + 1]


def unit_kernel(
    early, tensor_far, pair_ref, feat_ref, window_ref,
    kept_ref, total_ref, both_ref, gram_ref, tensor_ref, sems,
):
    kept = kept_ref.shape[0]
    places = [
        (j, kept_ref.at[j] if j < kept else tensor_ref.at[j - kept]) for j in range(early)
    ]
    copies = fetches(tensor_far, places, sems)
    start(copies[0:5])
    pair = pair_ref[0:128].astype(F32)
    mine, other = feat_ref[...], pair[0:64] + pair[64:128]
    first = lax.axis_index("tm") == 0
    feat = jnp.concatenate(
        [jnp.where(first, mine, other), jnp.where(first, other, mine)], axis=-1
    )
    gram = lax.dot_general(feat, feat, NT, precision=HIGH, preferred_element_type=F32)
    place = lax.broadcasted_iota(jnp.int32, (64, 64), 0) // 16 == lax.axis_index("unit") // 4
    gram = jnp.sum(jnp.where(place, gram, 0.0).reshape(4, 16, 64), axis=0)
    gram_ref[...] = split(gram, -1).astype(BF16)
    both_ref[...] = low(feat)
    feat = feat.astype(BF16)
    window = low(window_ref[...]).T
    start(copies[5:])
    for j in range(early):
        for copy in copies[j]:
            copy.wait()
        add_to(total_ref, by_unit_part(feat, places[j][1][...], window, j), j == 0)


def feature_kernel(
    early, tensor_far, kept_ref, gather_ref, both_ref, window_ref, by_unit_ref,
    sums_ref, send_ref, keep_ref, tensor_ref, unit_ref, total, unit_total, products, sems,
):
    windows, kept = tensor_far.shape[0], kept_ref.shape[0]
    order = [*range(early, windows), *range(kept, early)]
    places = [(j, tensor_ref.at[at]) for at, j in enumerate(order)]
    copies = fetches(tensor_far, places, sems)
    start(copies[0:4])
    left = lax.broadcasted_iota(jnp.int32, (32, 128), 1) < 64
    for at in range(0, 16, 2):
        one = gather_ref[at].astype(F32)
        two = gather_ref[at + 1].astype(F32)
        columns = pl.ds(at * 64, 128)
        unit_ref[0:32, columns] = jnp.where(left, one, pltpu.roll(two, 64, 1)).astype(BF16)
        unit_ref[32:64, columns] = jnp.where(left, pltpu.roll(one, 64, 1), two).astype(BF16)
    unit = unit_ref[...]
    gram = lax.dot_general(unit, unit, NT, preferred_element_type=F32)
    both = both_ref[...]
    feat = both.astype(BF16)
    window = low(window_ref[...]).T
    unit_total[...] = by_unit_ref[...]

    def add_window(j, slab, fresh):
        second = jnp.dot(unit, slab, preferred_element_type=F32)
        product = second * both
        products[j] = product[:, :128] + product[:, 128:]
        add_to(total, second * window[:, j : j + 1], fresh)

    for j in range(kept):
        add_window(j, kept_ref[j], j == 0)
    start(copies[4:8])
    for at, j in enumerate(order):
        for copy in copies[at]:
            copy.wait()
        if at == 3:
            start(copies[8:])
        slab = tensor_ref[at]
        add_window(j, slab, False)
        if j >= early:
            add_to(unit_total, by_unit_part(feat, slab, window, j), False)
    first = lax.axis_index("tm") == 0
    for at in range(0, 16, 2):
        top = unit_total[0:32, at * 64 : at * 64 + 128]
        bottom = unit_total[32:64, at * 64 : at * 64 + 128]
        even = jnp.where(left, top, pltpu.roll(bottom, 64, 1))
        odd = jnp.where(left, pltpu.roll(top, 64, 1), bottom)
        send_ref[at // 2] = jnp.where(first, odd, even).astype(BF16)
        keep_ref[at // 2] = jnp.where(first, even, odd)
    rest = jnp.concatenate([spread(gram), spread(jnp.sum(products[...], axis=-1))], axis=0)
    parts = [total[:, :128], total[:, 128:], split(rest, 0)]
    sums_ref[...] = jnp.concatenate(parts, axis=0).astype(BF16)


def add_four(refs):
    one, two, three, four = [ref[...].astype(F32) for ref in refs]
    return (one + two) + (three + four)


def near_kernel(
    s0, s1, s2, s3, by_unit_ref, other_unit_ref, gram_ref, scatter_ref, send_ref, keep_ref
):
    total = add_four((s0, s1, s2, s3))
    rest = total[128:168] + total[168:208]
    first = lax.axis_index("tm") == 0
    send_ref[...] = jnp.where(first, total[64:128], total[0:64])
    keep_ref[0:64] = jnp.where(first, total[0:64], total[64:128])
    keep_ref[64:96] = rest[0:32]
    by_window = split(rest[32:40], 0).astype(BF16)
    for at in range(8):
        by_unit = by_unit_ref[at] + other_unit_ref[at].astype(F32)
        scatter_ref[at, 0:32] = by_unit.astype(BF16)
        scatter_ref[at, 32:48] = by_window
        scatter_ref[at, 48:64] = gram_ref[...]


def pair_kernel(keep_ref, other_ref, sums_ref):
    sums_ref[0:64] = keep_ref[0:64] + other_ref[...]
    sums_ref[64:96] = keep_ref[64:96]


def group_kernel(scatter_ref, keep_ref, unit_ref, sums_ref):
    total = scatter_ref[0].astype(F32)
    for at in range(1, 8):
        total += scatter_ref[at].astype(F32)
    unit_ref[...] = total[0:32]
    gram = total[48:64]
    gram = jnp.concatenate([gram[:, :64] + gram[:, 64:]] * 4, axis=0)
    place = lax.broadcasted_iota(jnp.int32, (64, 64), 0) // 16 == lax.axis_index("unit") // 4
    gram = spread(jnp.where(place, gram, 0.0))
    rest = jnp.concatenate([keep_ref[64:96], gram, total[32:40] + total[40:48]], axis=0)
    sums_ref[...] = jnp.concatenate([keep_ref[0:64], split(rest, 0)], axis=0).astype(BF16)


def gradient_kernel(
    scales, s0, s1, s2, s3, by_unit_ref, unit_ref, window_ref, feat_ref, pair_ref,
    grad_unit_ref, grad_window_ref, grad_feat_ref,
):
    total = add_four((s0, s1, s2, s3))
    rest = total[64:136] + total[136:208]
    gram_unit, gram_feat = stack(rest[0:32]), stack(rest[32:64])
    window = window_ref[...]
    other = pair_ref[128:144, :].astype(F32)
    other = other[:, :64] + other[:, 64:]
    windows = jnp.concatenate([window, other], axis=0)
    gram_window = lax.dot_general(
        windows, windows, TN, precision=HIGH, preferred_element_type=F32
    )
    grad_unit_ref[...] = (
        dot(unit_ref[...], gram_window * gram_feat) - stack(by_unit_ref[...]).T
    ) * scales[0]
    grad_window_ref[...] = (
        dot(window, gram_unit * gram_feat) - stack(rest[64:72])
    ) * scales[1]
    grad_feat_ref[...] = (dot(gram_unit * gram_window, feat_ref[...]) - total[0:64]) * scales[2]


NEAR = (1, 2, 3)
FAR = (8, 6, 14)


def by_xor(value, mask):
    count = lax.axis_size("unit")
    return lax.ppermute(value, "unit", [(i, i ^ mask) for i in range(count)])


def other_windows(value):
    count = lax.axis_size("unit") * lax.axis_size("tm")
    return lax.ppermute(value, ("unit", "tm"), [(i, i ^ 17) for i in range(count)])


def body(tensor, unit_factor, window_factor, feat_factor):
    win_rows, unit_count, feat_count = tensor.shape
    units_all = unit_count * lax.axis_size("unit")
    windows_all = win_rows * lax.axis_size("tm")
    feats_all = feat_count * lax.axis_size("feat")
    shape = jax.ShapeDtypeStruct
    feat = feat_factor.T
    gather, pair, feat_near, window_near = call(
        prepare_kernel,
        [
            shape((16, 32, 128), BF16),
            shape((144, 128), BF16),
            shape((64, 128), F32),
            shape((win_rows, 64), F32),
        ],
        unit_factor, feat, window_factor,
        far=(0, 1, 2),
        scratch_shapes=[pltpu.VMEM((64, 64), F32), pltpu.SemaphoreType.DMA((3,))],
        name="prepare",
    )
    pair = other_windows(pair)
    gather = lax.all_to_all(gather.reshape(512, 128), GROUP, 0, 0, tiled=True).reshape(16, 32, 128)
    cost = pl.CostEstimate(flops=2**33, bytes_accessed=2**23, transcendentals=0)
    kept, early = 5, 9
    slabs = functools.partial(pltpu.VMEM, dtype=BF16)
    kept_windows, by_unit, both, gram = call(
        functools.partial(unit_kernel, early),
        [
            slabs((kept, unit_count, feat_count)),
            shape((64, unit_count), F32),
            shape((64, feat_count), F32),
            shape((16, 128), BF16),
        ],
        tensor, pair, feat_near, window_near,
        far=(0,),
        scratch_shapes=[
            slabs((early - kept, unit_count, feat_count)),
            pltpu.SemaphoreType.DMA((2 * early,)),
        ],
        cost_estimate=cost,
        name="by_unit",
    )
    sums, send, by_unit = call(
        functools.partial(feature_kernel, early),
        [shape((208, 128), BF16), shape((8, 32, 128), BF16), shape((8, 32, 128), F32)],
        tensor, pltpu.with_memory_space_constraint(kept_windows, pltpu.VMEM),
        gather, both, window_near, by_unit,
        far=(0,),
        scratch_shapes=[
            slabs((win_rows - kept, unit_count, feat_count)),
            pltpu.VMEM((64, unit_count), BF16),
            pltpu.VMEM((64, feat_count), F32),
            pltpu.VMEM((64, unit_count), F32),
            pltpu.VMEM((win_rows, 64, 128), F32),
            pltpu.SemaphoreType.DMA((2 * win_rows,)),
        ],
        cost_estimate=cost,
        name="by_feature",
    )
    other_unit = lax.ppermute(send, "tm", [(0, 1), (1, 0)])
    near = [by_xor(sums, mask) for mask in NEAR]
    scatter, send, keep = call(
        near_kernel,
        [shape((8, 64, 128), BF16), shape((64, 128), F32), shape((96, 128), F32)],
        sums, *near, by_unit, other_unit, gram,
        name="near_sums",
    )
    other = other_windows(send)
    scatter = lax.all_to_all(scatter.reshape(512, 128), "feat", 0, 0, tiled=True).reshape(8, 64, 128)
    keep = call(pair_kernel, shape((96, 128), F32), keep, other, name="pair_sums")
    by_unit, sums = call(
        group_kernel,
        [shape((32, 128), F32), shape((208, 128), BF16)],
        scatter, keep,
        name="group_sums",
    )
    far = [by_xor(sums, mask) for mask in FAR]
    scales = (
        1 / math.sqrt(windows_all * feats_all),
        1 / math.sqrt(units_all * feats_all),
        1 / math.sqrt(units_all * windows_all),
    )
    grad_unit, grad_window, grad_feat = call(
        functools.partial(gradient_kernel, scales),
        [shape((64, 64), F32), shape((win_rows, 64), F32), shape((64, 128), F32)],
        sums, *far, by_unit, unit_factor, window_factor, feat, pair,
        name="gradients",
    )
    return grad_unit, grad_window, grad_feat.T


def solution(mesh):
    in_specs = (
        P("tm", "unit", "feat"),
        P(("unit", "feat", "tm"), None),
        P("tm", None),
        P(("feat", "tm"), None),
    )
    out_specs = (P(("unit", "feat", "tm"), None), P("tm", None), P(("feat", "tm"), None))
    return jax.shard_map(body, mesh=mesh, in_specs=in_specs, out_specs=out_specs, check_vma=False)
```

```python
import functools
import math

import jax
import jax.numpy as jnp
from jax import lax
from jax.experimental import pallas as pl
from jax.experimental.pallas import tpu as pltpu
from jax.sharding import PartitionSpec as P

F32 = jnp.float32
BF16 = jnp.bfloat16
HIGH = lax.Precision.HIGHEST
NT = (((1,), (1,)), ((), ()))
TN = (((0,), (0,)), ((), ()))
GROUP = ("feat", "tm")
FAR = (8, 6, 14)
VMEM = pl.BlockSpec(memory_space=pltpu.VMEM)
HBM = pl.BlockSpec(memory_space=pltpu.HBM)


def call(kernel, out_shape, *args, name, far=(), **more):
    args = [
        pltpu.with_memory_space_constraint(arg, pltpu.HBM) if at in far else arg
        for at, arg in enumerate(args)
    ]
    return pl.pallas_call(
        kernel,
        out_shape=out_shape,
        in_specs=[HBM if at in far else VMEM for at in range(len(args))],
        out_specs=jax.tree.map(lambda _: VMEM, out_shape),
        compiler_params=pltpu.CompilerParams(vmem_limit_bytes=16 * 2**20),
        name=name,
        **more,
    )(*args)


def spread(rows):
    half = rows.shape[0] // 2
    return jnp.concatenate([rows[:half], rows[half:]], axis=-1)


def stack(rows):
    return jnp.concatenate([rows[:, :64], rows[:, 64:]], axis=0)


def low(value):
    return value.astype(BF16).astype(F32)


def split(value, axis):
    high_part = low(value)
    return jnp.concatenate([high_part, low(value - high_part)], axis=axis)


def dot(one, two):
    return jnp.dot(one, two, precision=HIGH, preferred_element_type=F32)


def fetches(tensor_far, places, sems):
    rows = tensor_far.shape[1] // 2
    result = []
    for at, (window, place) in enumerate(places):
        copies = []
        for part in range(2):
            span = pl.ds(part * rows, rows)
            source, target = tensor_far.at[window, span], place.at[span]
            copies.append(pltpu.make_async_copy(source, target, sems.at[2 * at + part]))
        result.append(copies)
    return result


def start(batch):
    for copies in batch:
        for copy in copies:
            copy.start()


def in_turn(steps):
    for step in steps:
        pl.when(lax.axis_index("tm") >= 0)(step)


def add_to(total, part, fresh):
    if fresh:
        total[...] = part
    else:
        total[...] += part


def by_unit_part(feat, slab, window, j):
    part = lax.dot_general(feat, slab, NT, preferred_element_type=F32)
    return part * window[:, j : j + 1]


def unit_kernel(
    early, tensor_far, other_ref, feat_far, window_far,
    kept_ref, total_ref, both_ref, gram_ref, window_ref, feat_ref, tensor_ref, sems, own_sems,
):
    own = [
        pltpu.make_async_copy(feat_far, feat_ref, own_sems.at[0]),
        pltpu.make_async_copy(window_far, window_ref, own_sems.at[1]),
    ]
    for copy in own:
        copy.start()
    kept = kept_ref.shape[0]
    places = [
        (j, kept_ref.at[j] if j < kept else tensor_ref.at[j - kept]) for j in range(early)
    ]
    copies = fetches(tensor_far, places, sems)
    start(copies[0:4])
    for copy in own:
        copy.wait()
    mine, other = feat_ref[...], other_ref[...]
    first = lax.axis_index("tm") == 0
    feat = jnp.concatenate(
        [jnp.where(first, mine, other), jnp.where(first, other, mine)], axis=-1
    )
    gram = lax.dot_general(feat, feat, NT, precision=HIGH, preferred_element_type=F32)
    place = lax.broadcasted_iota(jnp.int32, (64, 64), 0) // 16 == lax.axis_index("unit") // 4
    gram = jnp.sum(jnp.where(place, gram, 0.0).reshape(4, 16, 64), axis=0)
    gram_ref[...] = split(gram, -1).astype(BF16)
    both_ref[...] = low(feat)
    feat = feat.astype(BF16)
    window = low(window_ref[...]).T
    start(copies[4:])

    def some(first, last):
        for j in range(first, last):
            for copy in copies[j]:
                copy.wait()
        for j in range(first, last):
            add_to(total_ref, by_unit_part(feat, places[j][1][...], window, j), j == 0)

    in_turn([functools.partial(some, 0, 4), functools.partial(some, 4, early)])


def feature_kernel(
    early, tensor_far, kept_ref, gather_ref, both_ref, window_ref, by_unit_ref,
    sums_ref, send_ref, keep_ref, tensor_ref, unit_ref, total, unit_total, products, sems,
):
    windows, kept = tensor_far.shape[0], kept_ref.shape[0]
    order = [*range(early, windows), *range(kept, early)]
    places = [(j, tensor_ref.at[at]) for at, j in enumerate(order)]
    copies = fetches(tensor_far, places, sems)
    start(copies[0:4])
    left = lax.broadcasted_iota(jnp.int32, (32, 128), 1) < 64
    for at in range(0, 16, 2):
        rows = [stack(gather_ref[at].astype(F32)), stack(gather_ref[at + 1].astype(F32))]
        unit_ref[:, pl.ds(at * 64, 128)] = jnp.concatenate(rows, axis=0).T.astype(BF16)
    start(copies[4:8])
    unit = unit_ref[...]
    gram = lax.dot_general(unit, unit, NT, preferred_element_type=F32)
    both = both_ref[...]
    feat = both.astype(BF16)
    window = low(window_ref[...]).T
    unit_total[...] = by_unit_ref[...]

    def add_window(j, slab, fresh):
        second = jnp.dot(unit, slab, preferred_element_type=F32)
        product = second * both
        products[j] = product[:, :128] + product[:, 128:]
        add_to(total, second * window[:, j : j + 1], fresh)

    def held():
        start(copies[8:])
        for j in range(kept):
            add_window(j, kept_ref[j], j == 0)

    def some(first, last):
        for at in range(first, last):
            for copy in copies[at]:
                copy.wait()
        for at in range(first, last):
            slab, j = tensor_ref[at], order[at]
            add_window(j, slab, False)
            if j >= early:
                add_to(unit_total, by_unit_part(feat, slab, window, j), False)

    in_turn([held, functools.partial(some, 0, 5), functools.partial(some, 5, len(order))])
    first = lax.axis_index("tm") == 0
    for at in range(0, 16, 2):
        top = unit_total[0:32, at * 64 : at * 64 + 128]
        bottom = unit_total[32:64, at * 64 : at * 64 + 128]
        even = jnp.where(left, top, pltpu.roll(bottom, 64, 1))
        odd = jnp.where(left, pltpu.roll(top, 64, 1), bottom)
        send_ref[at // 2] = jnp.where(first, odd, even).astype(BF16)
        keep_ref[at // 2] = jnp.where(first, even, odd)
    rest = jnp.concatenate([spread(gram), spread(jnp.sum(products[...], axis=-1))], axis=0)
    parts = [total[:, :128], total[:, 128:], split(rest, 0)]
    sums_ref[...] = jnp.concatenate(parts, axis=0).astype(BF16)


def add_four(values):
    one, two, three, four = values
    return (one + two) + (three + four)


def join_kernel(s0, s1, sums_ref):
    total = s0[...].astype(F32) + s1[...].astype(F32)
    rest = split(total[128:168] + total[168:208], 0)
    sums_ref[...] = jnp.concatenate([total[0:128], rest], axis=0).astype(BF16)


def near_kernel(
    s0, s1, by_unit_ref, other_unit_ref, gram_ref, window_ref, scatter_ref, send_ref, keep_ref
):
    total = s0[...].astype(F32) + s1[...].astype(F32)
    rest = total[128:168] + total[168:208]
    first = lax.axis_index("tm") == 0
    send_ref[0:64] = jnp.where(first, total[64:128], total[0:64])
    send_ref[64:72] = spread(window_ref[...])
    keep_ref[0:64] = jnp.where(first, total[0:64], total[64:128])
    keep_ref[64:96] = rest[0:32]
    by_window = split(rest[32:40], 0).astype(BF16)
    for at in range(8):
        by_unit = by_unit_ref[at] + other_unit_ref[at].astype(F32)
        scatter_ref[at, 0:32] = by_unit.astype(BF16)
        scatter_ref[at, 32:48] = by_window
        scatter_ref[at, 48:64] = gram_ref[...]


def pair_kernel(keep_ref, other_ref, window_ref, sums_ref, gram_ref):
    windows = jnp.concatenate([window_ref[...], stack(other_ref[64:72])], axis=0)
    gram_ref[...] = lax.dot_general(
        windows, windows, TN, precision=HIGH, preferred_element_type=F32
    )
    sums_ref[0:64] = keep_ref[0:64] + other_ref[0:64]
    sums_ref[64:96] = keep_ref[64:96]


def group_kernel(scatter_ref, keep_ref, unit_ref, sums_ref):
    total = scatter_ref[0].astype(F32)
    for at in range(1, 8):
        total += scatter_ref[at].astype(F32)
    unit_ref[...] = total[0:32]
    gram = spread(total[48:64, :64] + total[48:64, 64:])
    rest = jnp.concatenate([keep_ref[64:96], total[32:40] + total[40:48], gram], axis=0)
    sums_ref[...] = jnp.concatenate([keep_ref[0:64], split(rest, 0)], axis=0).astype(BF16)


def gradient_kernel(
    scales, s0, s1, s2, s3, by_unit_ref, unit_ref, window_ref, feat_ref, gram_window_ref,
    grad_unit_ref, grad_window_ref, grad_feat_ref,
):
    parts = [ref[...].astype(F32) for ref in (s0, s1, s2, s3)]
    total = add_four(parts)
    rest = total[64:112] + total[112:160]
    gram_unit = stack(rest[0:32])
    gram_feat = jnp.zeros((64, 64), F32)
    place = lax.broadcasted_iota(jnp.int32, (64, 64), 0) // 16
    for part, mask in zip(parts, (0, *FAR)):
        rows = jnp.concatenate([stack(part[104:112] + part[152:160])] * 4, axis=0)
        gram_feat = jnp.where(place == (lax.axis_index("unit") ^ mask) // 4, rows, gram_feat)
    window = window_ref[...]
    gram_window = gram_window_ref[...]
    grad_unit_ref[...] = (
        dot(unit_ref[...], gram_window * gram_feat) - stack(by_unit_ref[...]).T
    ) * scales[0]
    grad_window_ref[...] = (
        dot(window, gram_unit * gram_feat) - stack(rest[32:40])
    ) * scales[1]
    grad_feat_ref[...] = (dot(gram_unit * gram_window, feat_ref[...]) - total[0:64]) * scales[2]


def by_xor(value, mask):
    count = lax.axis_size("unit")
    return lax.ppermute(value, "unit", [(i, i ^ mask) for i in range(count)])


def other_windows(value):
    count = lax.axis_size("unit") * lax.axis_size("tm")
    return lax.ppermute(value, ("unit", "tm"), [(i, i ^ 17) for i in range(count)])


def body(tensor, unit_factor, window_factor, feat_factor):
    win_rows, unit_count, feat_count = tensor.shape
    units_all = unit_count * lax.axis_size("unit")
    windows_all = win_rows * lax.axis_size("tm")
    feats_all = feat_count * lax.axis_size("feat")
    shape = jax.ShapeDtypeStruct
    feat = feat_factor.T
    gather = jnp.broadcast_to(spread(unit_factor.astype(BF16)), (16, 32, 128))
    gather = lax.all_to_all(gather.reshape(512, 128), GROUP, 0, 0, tiled=True).reshape(16, 32, 128)
    cost = pl.CostEstimate(flops=2**33, bytes_accessed=2**23, transcendentals=0)
    kept, early = 5, 8
    slabs = functools.partial(pltpu.VMEM, dtype=BF16)
    kept_windows, by_unit, both, gram, window_near = call(
        functools.partial(unit_kernel, early),
        [
            slabs((kept, unit_count, feat_count)),
            shape((64, unit_count), F32),
            shape((64, feat_count), F32),
            shape((16, 128), BF16),
            shape((win_rows, 64), F32),
        ],
        tensor, other_windows(feat), feat, window_factor,
        far=(0, 2, 3),
        scratch_shapes=[
            pltpu.VMEM((64, 128), F32),
            slabs((early - kept, unit_count, feat_count)),
            pltpu.SemaphoreType.DMA((2 * early,)),
            pltpu.SemaphoreType.DMA((2,)),
        ],
        cost_estimate=cost,
        name="by_unit",
    )
    sums, send, by_unit = call(
        functools.partial(feature_kernel, early),
        [shape((208, 128), BF16), shape((8, 32, 128), BF16), shape((8, 32, 128), F32)],
        tensor, pltpu.with_memory_space_constraint(kept_windows, pltpu.VMEM),
        gather, both, window_near, by_unit,
        far=(0,),
        scratch_shapes=[
            slabs((win_rows - kept, unit_count, feat_count)),
            pltpu.VMEM((64, unit_count), BF16),
            pltpu.VMEM((64, feat_count), F32),
            pltpu.VMEM((64, unit_count), F32),
            pltpu.VMEM((win_rows, 64, 128), F32),
            pltpu.SemaphoreType.DMA((2 * win_rows,)),
        ],
        cost_estimate=cost,
        name="by_feature",
    )
    other_unit = lax.ppermute(send, "tm", [(0, 1), (1, 0)])
    sums = call(join_kernel, shape((208, 128), BF16), sums, by_xor(sums, 1), name="pair_sums")
    scatter, send, keep = call(
        near_kernel,
        [shape((8, 64, 128), BF16), shape((72, 128), F32), shape((96, 128), F32)],
        sums, by_xor(sums, 2), by_unit, other_unit, gram, window_near,
        name="near_sums",
    )
    other = other_windows(send)
    scatter = lax.all_to_all(scatter.reshape(512, 128), "feat", 0, 0, tiled=True).reshape(8, 64, 128)
    keep, gram_window = call(
        pair_kernel,
        [shape((96, 128), F32), shape((64, 64), F32)],
        keep, other, window_near,
        name="other_sums",
    )
    by_unit, sums = call(
        group_kernel,
        [shape((32, 128), F32), shape((160, 128), BF16)],
        scatter, keep,
        name="group_sums",
    )
    far = [by_xor(sums, mask) for mask in FAR]
    scales = (
        1 / math.sqrt(windows_all * feats_all),
        1 / math.sqrt(units_all * feats_all),
        1 / math.sqrt(units_all * windows_all),
    )
    grad_unit, grad_window, grad_feat = call(
        functools.partial(gradient_kernel, scales),
        [shape((64, 64), F32), shape((win_rows, 64), F32), shape((64, 128), F32)],
        sums, *far, by_unit, unit_factor, window_factor, feat, gram_window,
        name="gradients",
    )
    return grad_unit, grad_window, grad_feat.T


def solution(mesh):
    in_specs = (
        P("tm", "unit", "feat"),
        P(("unit", "feat", "tm"), None),
        P("tm", None),
        P(("feat", "tm"), None),
    )
    out_specs = (P(("unit", "feat", "tm"), None), P("tm", None), P(("feat", "tm"), None))
    return jax.shard_map(body, mesh=mesh, in_specs=in_specs, out_specs=out_specs, check_vma=False)
```

```python
import functools
import math

import jax
import jax.numpy as jnp
from jax import lax
from jax.experimental import pallas as pl
from jax.experimental.pallas import tpu as pltpu
from jax.sharding import PartitionSpec as P

F32 = jnp.float32
BF16 = jnp.bfloat16
HIGH = lax.Precision.HIGHEST
NT = (((1,), (1,)), ((), ()))
TN = (((0,), (0,)), ((), ()))
GROUP = ("feat", "tm")
ORDER = [*range(12, 16), *range(12)]
FAR = (8, 6, 14)
VMEM = pl.BlockSpec(memory_space=pltpu.VMEM)
HBM = pl.BlockSpec(memory_space=pltpu.HBM)


def call(kernel, out_shape, *args, name, far=(), **more):
    args = [
        pltpu.with_memory_space_constraint(arg, pltpu.HBM) if at in far else arg
        for at, arg in enumerate(args)
    ]
    return pl.pallas_call(
        kernel,
        out_shape=out_shape,
        in_specs=[HBM if at in far else VMEM for at in range(len(args))],
        out_specs=jax.tree.map(lambda _: VMEM, out_shape),
        compiler_params=pltpu.CompilerParams(vmem_limit_bytes=16 * 2**20),
        name=name,
        **more,
    )(*args)


def spread(rows):
    half = rows.shape[0] // 2
    return jnp.concatenate([rows[:half], rows[half:]], axis=-1)


def stack(rows):
    return jnp.concatenate([rows[:, :64], rows[:, 64:]], axis=0)


def low(value):
    return value.astype(BF16).astype(F32)


def split(value, axis):
    high_part = low(value)
    return jnp.concatenate([high_part, low(value - high_part)], axis=axis)


def dot(one, two):
    return jnp.dot(one, two, precision=HIGH, preferred_element_type=F32)


def fetches(tensor_far, places, sems):
    rows = tensor_far.shape[1] // 2
    result = []
    for at, (window, place) in enumerate(places):
        copies = []
        for part in range(2):
            span = pl.ds(part * rows, rows)
            source, target = tensor_far.at[window, span], place.at[span]
            copies.append(pltpu.make_async_copy(source, target, sems.at[2 * at + part]))
        result.append(copies)
    return result


def start(batch):
    for copies in batch:
        for copy in copies:
            copy.start()


def in_turn(steps):
    for step in steps:
        pl.when(lax.axis_index("tm") >= 0)(step)


def add_to(total, part, fresh):
    if fresh:
        total[...] = part
    else:
        total[...] += part


def by_unit_part(feat, slab, window, j):
    part = lax.dot_general(feat, slab, NT, preferred_element_type=F32)
    return part * window[:, j : j + 1]


def unit_kernel(
    early, tensor_far, other_ref, feat_far, window_far,
    kept_ref, total_ref, both_ref, gram_ref, window_ref, feat_ref, tensor_ref, sems, own_sems,
):
    own = [
        pltpu.make_async_copy(feat_far, feat_ref, own_sems.at[0]),
        pltpu.make_async_copy(window_far, window_ref, own_sems.at[1]),
    ]
    for copy in own:
        copy.start()
    kept = kept_ref.shape[0]
    places = [
        (j, kept_ref.at[j] if j < kept else tensor_ref.at[j - kept]) for j in range(early)
    ]
    copies = fetches(tensor_far, places, sems)
    start(copies[0:4])
    for copy in own:
        copy.wait()
    mine, other = feat_ref[...], other_ref[...]
    first = lax.axis_index("tm") == 0
    feat = jnp.concatenate(
        [jnp.where(first, mine, other), jnp.where(first, other, mine)], axis=-1
    )
    gram = lax.dot_general(feat, feat, NT, precision=HIGH, preferred_element_type=F32)
    place = lax.broadcasted_iota(jnp.int32, (64, 64), 0) // 16 == lax.axis_index("unit") // 4
    gram = jnp.sum(jnp.where(place, gram, 0.0).reshape(4, 16, 64), axis=0)
    gram_ref[...] = split(gram, -1).astype(BF16)
    both_ref[...] = low(feat)
    feat = feat.astype(BF16)
    window = low(window_ref[...]).T
    start(copies[4:])

    def some(first, last):
        for j in range(first, last):
            for copy in copies[j]:
                copy.wait()
        for j in range(first, last):
            add_to(total_ref, by_unit_part(feat, places[j][1][...], window, j), j == 0)

    in_turn([functools.partial(some, 0, 4), functools.partial(some, 4, early)])


def feature_kernel(
    early, tensor_far, kept_ref, gather_ref, both_ref, window_ref, by_unit_ref,
    sums_ref, send_ref, keep_ref, tensor_ref, unit_ref, total, unit_total, products, sems,
):
    windows, kept = tensor_far.shape[0], kept_ref.shape[0]
    order = [*range(early, windows), *range(kept, early)]
    places = [(j, tensor_ref.at[at]) for at, j in enumerate(order)]
    copies = fetches(tensor_far, places, sems)
    start(copies[0:4])
    left = lax.broadcasted_iota(jnp.int32, (32, 128), 1) < 64
    for at in range(0, 16, 2):
        rows = [stack(gather_ref[ORDER.index(at + k)].astype(F32)) for k in range(2)]
        unit_ref[:, pl.ds(at * 64, 128)] = jnp.concatenate(rows, axis=0).T.astype(BF16)
    start(copies[4:8])
    unit = unit_ref[...]
    gram = lax.dot_general(unit, unit, NT, preferred_element_type=F32)
    both = both_ref[...]
    feat = both.astype(BF16)
    window = low(window_ref[...]).T
    unit_total[...] = by_unit_ref[...]

    def add_window(j, slab, fresh):
        second = jnp.dot(unit, slab, preferred_element_type=F32)
        product = second * both
        products[j] = product[:, :128] + product[:, 128:]
        add_to(total, second * window[:, j : j + 1], fresh)

    def held():
        start(copies[8:])
        for j in range(kept):
            add_window(j, kept_ref[j], j == 0)

    def some(first, last):
        for at in range(first, last):
            for copy in copies[at]:
                copy.wait()
        for at in range(first, last):
            slab, j = tensor_ref[at], order[at]
            add_window(j, slab, False)
            if j >= early:
                add_to(unit_total, by_unit_part(feat, slab, window, j), False)

    in_turn([held, functools.partial(some, 0, 5), functools.partial(some, 5, len(order))])
    first = lax.axis_index("tm") == 0
    for at in range(0, 16, 2):
        top = unit_total[0:32, at * 64 : at * 64 + 128]
        bottom = unit_total[32:64, at * 64 : at * 64 + 128]
        even = jnp.where(left, top, pltpu.roll(bottom, 64, 1))
        odd = jnp.where(left, pltpu.roll(top, 64, 1), bottom)
        send_ref[at // 2] = jnp.where(first, odd, even).astype(BF16)
        keep_ref[at // 2] = jnp.where(first, even, odd)
    rest = jnp.concatenate([spread(gram), spread(jnp.sum(products[...], axis=-1))], axis=0)
    parts = [total[:, :128], total[:, 128:], split(rest, 0)]
    sums_ref[...] = jnp.concatenate(parts, axis=0).astype(BF16)


def add_four(values):
    one, two, three, four = values
    return (one + two) + (three + four)


def join_kernel(s0, s1, sums_ref):
    total = s0[...].astype(F32) + s1[...].astype(F32)
    rest = split(total[128:168] + total[168:208], 0)
    sums_ref[...] = jnp.concatenate([total[0:128], rest], axis=0).astype(BF16)


def near_kernel(
    s0, s1, by_unit_ref, other_unit_ref, gram_ref, window_ref, scatter_ref, send_ref, keep_ref
):
    total = s0[...].astype(F32) + s1[...].astype(F32)
    rest = total[128:168] + total[168:208]
    first = lax.axis_index("tm") == 0
    send_ref[0:64] = jnp.where(first, total[64:128], total[0:64])
    send_ref[64:72] = spread(window_ref[...])
    keep_ref[0:64] = jnp.where(first, total[0:64], total[64:128])
    keep_ref[64:96] = rest[0:32]
    by_window = split(rest[32:40], 0).astype(BF16)
    for at in range(8):
        by_unit = by_unit_ref[at] + other_unit_ref[at].astype(F32)
        scatter_ref[at, 0:32] = by_unit.astype(BF16)
        scatter_ref[at, 32:48] = by_window
        scatter_ref[at, 48:64] = gram_ref[...]


def pair_kernel(keep_ref, other_ref, window_ref, sums_ref, gram_ref):
    windows = jnp.concatenate([window_ref[...], stack(other_ref[64:72])], axis=0)
    gram_ref[...] = lax.dot_general(
        windows, windows, TN, precision=HIGH, preferred_element_type=F32
    )
    sums_ref[0:64] = keep_ref[0:64] + other_ref[0:64]
    sums_ref[64:96] = keep_ref[64:96]


def group_kernel(scatter_ref, keep_ref, unit_ref, sums_ref):
    total = scatter_ref[0].astype(F32)
    for at in range(1, 8):
        total += scatter_ref[at].astype(F32)
    unit_ref[...] = total[0:32]
    gram = spread(total[48:64, :64] + total[48:64, 64:])
    rest = jnp.concatenate([keep_ref[64:96], total[32:40] + total[40:48], gram], axis=0)
    sums_ref[...] = jnp.concatenate([keep_ref[0:64], split(rest, 0)], axis=0).astype(BF16)


def gradient_kernel(
    scales, s0, s1, s2, s3, by_unit_ref, unit_ref, window_ref, feat_ref, gram_window_ref,
    grad_unit_ref, grad_window_ref, grad_feat_ref,
):
    parts = [ref[...].astype(F32) for ref in (s0, s1, s2, s3)]
    total = add_four(parts)
    rest = total[64:112] + total[112:160]
    gram_unit = stack(rest[0:32])
    gram_feat = jnp.zeros((64, 64), F32)
    place = lax.broadcasted_iota(jnp.int32, (64, 64), 0) // 16
    for part, mask in zip(parts, (0, *FAR)):
        rows = jnp.concatenate([stack(part[104:112] + part[152:160])] * 4, axis=0)
        gram_feat = jnp.where(place == (lax.axis_index("unit") ^ mask) // 4, rows, gram_feat)
    window = window_ref[...]
    gram_window = gram_window_ref[...]
    grad_unit_ref[...] = (
        dot(unit_ref[...], gram_window * gram_feat) - stack(by_unit_ref[...]).T
    ) * scales[0]
    grad_window_ref[...] = (
        dot(window, gram_unit * gram_feat) - stack(rest[32:40])
    ) * scales[1]
    grad_feat_ref[...] = (dot(gram_unit * gram_window, feat_ref[...]) - total[0:64]) * scales[2]


def by_xor(value, mask):
    count = lax.axis_size("unit")
    return lax.ppermute(value, "unit", [(i, i ^ mask) for i in range(count)])


def other_windows(value):
    count = lax.axis_size("unit") * lax.axis_size("tm")
    return lax.ppermute(value, ("unit", "tm"), [(i, i ^ 17) for i in range(count)])


def body(tensor, unit_factor, window_factor, feat_factor):
    win_rows, unit_count, feat_count = tensor.shape
    units_all = unit_count * lax.axis_size("unit")
    windows_all = win_rows * lax.axis_size("tm")
    feats_all = feat_count * lax.axis_size("feat")
    shape = jax.ShapeDtypeStruct
    feat = feat_factor.T
    gather = jnp.broadcast_to(spread(unit_factor.astype(BF16)), (16, 32, 128))
    gather = lax.all_to_all(gather.reshape(512, 128), GROUP, 0, 0, tiled=True, axis_index_groups=[ORDER]).reshape(16, 32, 128)
    cost = pl.CostEstimate(flops=2**33, bytes_accessed=2**23, transcendentals=0)
    kept, early = 5, 8
    slabs = functools.partial(pltpu.VMEM, dtype=BF16)
    kept_windows, by_unit, both, gram, window_near = call(
        functools.partial(unit_kernel, early),
        [
            slabs((kept, unit_count, feat_count)),
            shape((64, unit_count), F32),
            shape((64, feat_count), F32),
            shape((16, 128), BF16),
            shape((win_rows, 64), F32),
        ],
        tensor, other_windows(feat), feat, window_factor,
        far=(0, 2, 3),
        scratch_shapes=[
            pltpu.VMEM((64, 128), F32),
            slabs((early - kept, unit_count, feat_count)),
            pltpu.SemaphoreType.DMA((2 * early,)),
            pltpu.SemaphoreType.DMA((2,)),
        ],
        cost_estimate=cost,
        name="by_unit",
    )
    sums, send, by_unit = call(
        functools.partial(feature_kernel, early),
        [shape((208, 128), BF16), shape((8, 32, 128), BF16), shape((8, 32, 128), F32)],
        tensor, pltpu.with_memory_space_constraint(kept_windows, pltpu.VMEM),
        gather, both, window_near, by_unit,
        far=(0,),
        scratch_shapes=[
            slabs((win_rows - kept, unit_count, feat_count)),
            pltpu.VMEM((64, unit_count), BF16),
            pltpu.VMEM((64, feat_count), F32),
            pltpu.VMEM((64, unit_count), F32),
            pltpu.VMEM((win_rows, 64, 128), F32),
            pltpu.SemaphoreType.DMA((2 * win_rows,)),
        ],
        cost_estimate=cost,
        name="by_feature",
    )
    other_unit = lax.ppermute(send, "tm", [(0, 1), (1, 0)])
    sums = call(join_kernel, shape((208, 128), BF16), sums, by_xor(sums, 1), name="pair_sums")
    scatter, send, keep = call(
        near_kernel,
        [shape((8, 64, 128), BF16), shape((72, 128), F32), shape((96, 128), F32)],
        sums, by_xor(sums, 2), by_unit, other_unit, gram, window_near,
        name="near_sums",
    )
    other = other_windows(send)
    scatter = lax.all_to_all(scatter.reshape(512, 128), "feat", 0, 0, tiled=True).reshape(8, 64, 128)
    keep, gram_window = call(
        pair_kernel,
        [shape((96, 128), F32), shape((64, 64), F32)],
        keep, other, window_near,
        name="other_sums",
    )
    by_unit, sums = call(
        group_kernel,
        [shape((32, 128), F32), shape((160, 128), BF16)],
        scatter, keep,
        name="group_sums",
    )
    far = [by_xor(sums, mask) for mask in FAR]
    scales = (
        1 / math.sqrt(windows_all * feats_all),
        1 / math.sqrt(units_all * feats_all),
        1 / math.sqrt(units_all * windows_all),
    )
    grad_unit, grad_window, grad_feat = call(
        functools.partial(gradient_kernel, scales),
        [shape((64, 64), F32), shape((win_rows, 64), F32), shape((64, 128), F32)],
        sums, *far, by_unit, unit_factor, window_factor, feat, gram_window,
        name="gradients",
    )
    return grad_unit, grad_window, grad_feat.T


def solution(mesh):
    in_specs = (
        P("tm", "unit", "feat"),
        P(("unit", "feat", "tm"), None),
        P("tm", None),
        P(("feat", "tm"), None),
    )
    out_specs = (P(("unit", "feat", "tm"), None), P("tm", None), P(("feat", "tm"), None))
    return jax.shard_map(body, mesh=mesh, in_specs=in_specs, out_specs=out_specs, check_vma=False)
```
